256 devices in a mesh: occ: 8 (over z), vir: 16 (over x, y), stream: 2 (over core).
Axes of the slice: x: 4, y: 4, z: 8, core: 2. Of those that a mesh axis runs over, the one named last changes fastest.
Arguments:
- doubles: bfloat16 [3072, 32, 1024], P('occ', 'vir'), may hold values from -6 to 6
- integrals: bfloat16 [16, 2, 2, 2, 1024, 1024], P('vir', 'stream'), may hold values from -0.09375 to 0.09375
- tiles: int32 [16, 2, 2], P('vir', 'stream'), may hold values from 0 to 31, as said below
Outputs:
- ladder: bfloat16 [3072, 32, 1024], P('occ', ('vir', 'stream'))
The draws below stay inside these ranges and needn't reach their ends.
Inputs may be any that keep to these rules, and one draw needn't show every extreme that they name: tiles[j, k, 0] // 2 equals (j - 1) mod 16 and tiles[j, k, 1] // 2 equals (j + 8) mod 16: slot 0 of vir index j uses a tile pair held by the vir index before it, slot 1 one held by the vir index half the axis away; which of its 2 tile pairs is drawn.
All inputs are finite; a program needn't handle non-finite values.
Results may differ from the reference program's by a relative error of at most 0.001.
Values may be sent and summed in bfloat16 or wider, within the bound.
No kernel may reach another device: no remote copies, remote signals or barrier semaphores. Data moves between devices by JAX's collectives and lax.ppermute only.
A program may use at most 128 MiB of HBM per device.

```python
import jax
import jax.numpy as jnp
from jax import lax

PAIR = 1024
CD_DEV = 2
OCC = 3072
NCD = 32
N_VIR = 16
N_STREAM = 2


def draw_tiles(key, part):
    key = jax.random.fold_in(key, 7)
    vir_index = jnp.arange(N_VIR, dtype=jnp.int32)[:, None, None]
    slot_index = jnp.arange(2, dtype=jnp.int32)[None, None, :]
    owners = (vir_index - 1 + slot_index * (N_VIR // 2 + 1) + N_VIR) % N_VIR
    owners = jnp.broadcast_to(owners, (N_VIR, N_STREAM, 2))
    local = jax.random.randint(key, (N_VIR, N_STREAM, 2), 0, CD_DEV)
    first = (vir_index == 0) & (slot_index == 0)
    local = jnp.where(first, CD_DEV - 1, local)
    second = (vir_index == 1) & (slot_index == 0)
    local = jnp.where(second, 0, local)
    return (owners * CD_DEV + local).astype(jnp.int32)


def shard_levels(stream_key, dims, shards, low, high):
    loudness, own = 1.0, jax.random.fold_in(stream_key, 6)
    for dim, parts in shards:
        heights = jnp.exp(jax.random.uniform(jax.random.fold_in(own, dim), (parts,), jnp.float32, low / len(shards), high / len(shards)))
        loudness = loudness * jnp.repeat(heights, dims[dim] // parts).reshape([-1 if axis == dim else 1 for axis in range(len(dims))])
    return loudness


def gaussian(rng, dims, scale, most, shards=(), kind=jnp.bfloat16):
    values = jax.random.normal(rng, dims, jnp.float32) * scale
    if len(shards) > 0:
        values = shard_levels(rng, dims, shards, -0.22, 0.18) * values
    return jnp.clip(values, min=-most, max=most).astype(kind)


def setup_inputs(seed: int = 0) -> dict:
    seeds = jax.random.split(jax.random.key(seed), 4)
    return {
        "doubles": gaussian(seeds[0], (OCC, NCD, PAIR), 1.0, 6.0, ((0, 8), (1, 16))),
        "integrals": gaussian(seeds[1], (N_VIR, N_STREAM, N_STREAM, 2, PAIR, PAIR), (2 * N_STREAM * PAIR) ** -0.5, 0.09375, ((0, 16), (1, 2))),
        "tiles": draw_tiles(jax.random.fold_in(seeds[3], 71), 0),
    }


def reference(doubles, integrals, tiles):
    def one_vir(index):
        blocks = integrals[index]
        used = tiles[index]
        results = []
        for tile_a in range(N_STREAM):
            total = jnp.zeros((OCC, PAIR), jnp.float32)
            for holder in range(N_STREAM):
                for slot in range(2):
                    picked = jnp.take(doubles, used[holder, slot], axis=1)
                    total = total + lax.dot_general(picked, blocks[holder, tile_a, slot], (((1,), (1,)), ((), ())), preferred_element_type=jnp.float32)
            results.append(total)
        return jnp.stack(results, 0)

    stacked = lax.map(one_vir, jnp.arange(N_VIR, dtype=jnp.int32))
    return jnp.transpose(stacked, (2, 0, 1, 3)).reshape(OCC, N_VIR * N_STREAM, PAIR).astype(jnp.bfloat16)
```

```python
import jax
import jax.numpy as jnp
from jax import lax
from jax.sharding import PartitionSpec as P

SWAP = ((0, 1), (1, 0))


def shift(step):
    return [(j, (j + step) % 16) for j in range(16)]


def swap(value):
    return lax.ppermute(value, "stream", SWAP)


def on_device(doubles, integrals, tiles):
    core = lax.axis_index("stream")
    mine = lax.dynamic_index_in_dim(doubles, core, 1, keepdims=False)
    first = lax.ppermute(mine, "vir", shift(1))
    second = lax.ppermute(mine, "vir", shift(8))
    used = tiles[0, 0]
    other_used = swap(used)
    blocks = integrals[0, 0]
    kept = lax.dynamic_index_in_dim(blocks, core, 0, keepdims=False)
    got = swap(lax.dynamic_index_in_dim(blocks, 1 - core, 0, keepdims=False))
    total = 0
    for slot, held in enumerate((first, second)):
        other = swap(held)
        for use, block in ((used[slot], kept[slot]), (other_used[slot], got[slot])):
            picked = jnp.where(use % 2 == core, held, other)
            total = total + lax.dot_general(
                picked, block, (((1,), (1,)), ((), ())), preferred_element_type=jnp.float32
            )
    return total.astype(jnp.bfloat16)[:, None]


def solution(mesh):
    placed = (
        P("occ", "vir", None),
        P("vir", "stream", None, None, None, None),
        P("vir", "stream", None),
    )
    return jax.shard_map(
        on_device,
        mesh=mesh,
        in_specs=placed,
        out_specs=P("occ", ("vir", "stream"), None),
        check_vma=False,
    )
```

```python
import functools

import jax
import jax.numpy as jnp
from jax import lax
from jax.experimental import pallas as pl
from jax.experimental.pallas import tpu as pltpu
from jax.sharding import PartitionSpec as P

SWAP = ((0, 1), (1, 0))
CUT = 384
BUSY = 0
HOLD = 4600*10**6
TRANSPOSED = (((1,), (1,)), ((), ()))


def device(x, y, core):
    return ((x % 4) * 4 + y % 4) * 2 + core


def chips():
    return [(x, y) for x in range(4) for y in range(4)]


def route(pairs):
    return tuple((device(*a), device(*b)) for a, b in pairs)


ACROSS = route(((x, y, c), (x + 2, y, c)) for x, y in chips() for c in (0, 1))
WRAP = [((x, 3, c), (x + 1, 0, c)) for x in range(4) for c in (0, 1)]
INSIDE = [((x, y, c), (x, y + 1, c)) for x, y in chips() for c in (0, 1) if y < 3]
NEXT = route(INSIDE + WRAP)
NEXT_INSIDE = route(INSIDE)
RELAY_ROW = {0: 1, 1: 0}
RELAY_Y = route(((x, 3, c), (x, RELAY_ROW[c], c)) for x in range(4) for c in (0, 1))
RELAY_X = route(((x, RELAY_ROW[c], c), (x + 1, 0, c)) for x in range(4) for c in (0, 1))


def swap(value):
    return lax.ppermute(value, "stream", SWAP)


def send(value, pairs):
    return lax.ppermute(value, ("vir", "stream"), pairs)


VMEM = pl.BlockSpec(memory_space=pltpu.VMEM)
SMEM = pl.BlockSpec(memory_space=pltpu.SMEM)
ANYWHERE = pl.BlockSpec(memory_space=pl.ANY)


def params(mebibytes):
    return pltpu.CompilerParams(vmem_limit_bytes=mebibytes * 2**20)


def load_kernel(blocks, got, weights, arrived):
    core = lax.axis_index("stream")
    copies = [
        pltpu.make_async_copy(whole.at[core], weights.at[holder], arrived.at[holder])
        for holder, whole in enumerate((blocks, got))
    ]
    for copy in copies:
        copy.start()
    for copy in copies:
        copy.wait()


def load(blocks, got):
    hbm = pl.BlockSpec(memory_space=pltpu.HBM)
    return pl.pallas_call(
        load_kernel,
        out_shape=jax.ShapeDtypeStruct((2, 2, 1024, 1024), blocks.dtype),
        in_specs=[hbm, hbm],
        out_specs=VMEM,
        scratch_shapes=[pltpu.SemaphoreType.DMA((2,))],
        compiler_params=params(1),
    )(blocks, got)


def choose_kernel(inside, relayed, out, arrived):
    row = lax.axis_index("vir") % 4

    def move(source):
        copy = pltpu.make_async_copy(source, out, arrived)
        copy.start()
        copy.wait()

    @pl.when(row != 0)
    def _():
        move(inside)

    @pl.when(row == 0)
    def _():
        move(relayed)


def choose(inside, relayed):
    return pl.pallas_call(
        choose_kernel,
        out_shape=jax.ShapeDtypeStruct(inside.shape, inside.dtype),
        in_specs=[ANYWHERE] * 2,
        out_specs=VMEM,
        scratch_shapes=[pltpu.SemaphoreType.DMA],
        compiler_params=params(1),
    )(inside, relayed)


def hold_kernel(*refs):
    pass


def hold(*values, flops):
    return pl.pallas_call(
        hold_kernel,
        out_shape=[jax.ShapeDtypeStruct(value.shape, value.dtype) for value in values],
        in_specs=[ANYWHERE] * len(values),
        out_specs=[ANYWHERE] * len(values),
        input_output_aliases={i: i for i in range(len(values))},
        cost_estimate=pl.CostEstimate(flops=flops, bytes_accessed=0, transcendentals=0),
        compiler_params=params(1),
    )(*values)


def add_kernel(places, has_total, flags, weights, *refs):
    total = refs[-2][...] if has_total else None
    out = refs[-1]
    for holder in (0, 1):
        for i, (slot, low, high) in enumerate(places):
            held, other = refs[2 * i], refs[2 * i + 1]
            picked = jnp.where(flags[holder * 2 + slot] == 1, held[...], other[...])
            block = weights[holder, slot, :, low:high]
            term = lax.dot_general(picked, block, TRANSPOSED, preferred_element_type=jnp.float32)
            total = term if total is None else total + term
    out[...] = total.astype(out.dtype)


def add_parts(flags, weights, parts, total=None, dtype=jnp.float32, flops=0):
    operands = [flags, weights]
    for part in parts:
        operands += part[3:]
    if total is not None:
        operands.append(total)
    return pl.pallas_call(
        functools.partial(add_kernel, tuple(part[:3] for part in parts), total is not None),
        out_shape=jax.ShapeDtypeStruct((parts[0][3].shape[0], 1024), dtype),
        in_specs=[SMEM] + [VMEM] * (len(operands) - 1),
        out_specs=VMEM,
        cost_estimate=pl.CostEstimate(flops=flops, bytes_accessed=0, transcendentals=0),
        compiler_params=params(12),
    )(*operands)


def on_device(doubles, integrals, tiles):
    core = lax.axis_index("stream")
    mine = lax.dynamic_index_in_dim(doubles, core, 1, keepdims=False)
    left, right = mine[:, :CUT], mine[:, CUT:]
    across = send(mine, ACROSS)
    relayed = send(send(right, RELAY_Y), RELAY_X)
    inside = send(right, NEXT_INSIDE)
    first_left = send(left, NEXT)

    blocks, _ = lax.optimization_barrier((integrals[0, 0], mine))
    got, tiles = lax.optimization_barrier((swap(blocks), tiles))
    weights = load(blocks, got)
    used = tiles[0, 0]
    all_used = jnp.concatenate([used, swap(used)])
    flags = (all_used % 2 == core).astype(jnp.int32)

    across, inside, weights, flags = lax.optimization_barrier((across, inside, weights, flags))
    first_right = choose(inside, relayed)
    total = add_parts(flags, weights, [(1, 0, 1024, across, swap(across))], flops=BUSY)
    first_left, other_left = hold(first_left, swap(first_left), flops=HOLD)
    out = add_parts(
        flags,
        weights,
        [
            (0, 0, CUT, first_left, other_left),
            (0, CUT, 1024, first_right, swap(first_right)),
        ],
        total,
        jnp.bfloat16,
    )
    return out[:, None]


def solution(mesh):
    placed = (
        P("occ", "vir", None),
        P("vir", "stream", None, None, None, None),
        P("vir", "stream", None),
    )
    return jax.shard_map(
        on_device,
        mesh=mesh,
        in_specs=placed,
        out_specs=P("occ", ("vir", "stream"), None),
        check_vma=False,
    )
```

```python
import functools

import jax
import jax.numpy as jnp
from jax import lax
from jax.experimental import pallas as pl
from jax.experimental.pallas import tpu as pltpu
from jax.sharding import PartitionSpec as P

SWAP = ((0, 1), (1, 0))
CUT = 256
SEPARATE = 4600 * 10**6
HOLD = 4600 * 10**6
TRANSPOSED = (((1,), (1,)), ((), ()))


def device(x, y, core):
    return ((x % 4) * 4 + y % 4) * 2 + core


def chips():
    return [(x, y) for x in range(4) for y in range(4)]


def route(pairs):
    return tuple((device(*a), device(*b)) for a, b in pairs)


ACROSS = route(((x, y, c), (x + 2, y, c)) for x, y in chips() for c in (0, 1))
WRAP = [((x, 3, c), (x + 1, 0, c)) for x in range(4) for c in (0, 1)]
INSIDE = [((x, y, c), (x, y + 1, c)) for x, y in chips() for c in (0, 1) if y < 3]
NEXT = route(INSIDE + WRAP)
NEXT_INSIDE = route(INSIDE)
RELAY_ROW = {0: 1, 1: 0}
RELAY_Y = route(((x, 3, c), (x, RELAY_ROW[c], c)) for x in range(4) for c in (0, 1))
RELAY_X = route(((x, RELAY_ROW[c], c), (x + 1, 0, c)) for x in range(4) for c in (0, 1))


def swap(value):
    return lax.ppermute(value, "stream", SWAP)


def send(value, pairs):
    return lax.ppermute(value, ("vir", "stream"), pairs)


VMEM = pl.BlockSpec(memory_space=pltpu.VMEM)
SMEM = pl.BlockSpec(memory_space=pltpu.SMEM)
ANYWHERE = pl.BlockSpec(memory_space=pl.ANY)


def params(mebibytes):
    return pltpu.CompilerParams(vmem_limit_bytes=mebibytes * 2**20)


def in_hbm(value):
    return pltpu.with_memory_space_constraint(value, pltpu.HBM)


def cut_kernel(doubles, out, arrived):
    rows = out.shape[0]
    core = lax.axis_index("stream")
    copy = pltpu.make_async_copy(doubles.at[pl.ds(core * rows, rows)], out, arrived)
    copy.start()
    copy.wait()


def cut_rows(doubles):
    shape = (doubles.shape[0] // 2, *doubles.shape[1:])
    return pl.pallas_call(
        cut_kernel,
        out_shape=jax.ShapeDtypeStruct(shape, doubles.dtype),
        in_specs=[pl.BlockSpec(memory_space=pltpu.HBM)],
        out_specs=VMEM,
        scratch_shapes=[pltpu.SemaphoreType.DMA],
        compiler_params=params(1),
    )(in_hbm(doubles))


def take_kernel(doubles, left, right):
    def take_pair(pair):
        left[...] = doubles[:, pair, :CUT]
        right[...] = doubles[:, pair, CUT:]

    @pl.when(lax.axis_index("stream") == 0)
    def _():
        take_pair(0)

    @pl.when(lax.axis_index("stream") == 1)
    def _():
        take_pair(1)


def take(doubles):
    rows, _, width = doubles.shape
    return pl.pallas_call(
        take_kernel,
        out_shape=[
            jax.ShapeDtypeStruct((rows, columns), doubles.dtype) for columns in (CUT, width - CUT)
        ],
        in_specs=[VMEM],
        out_specs=[VMEM] * 2,
        cost_estimate=pl.CostEstimate(flops=0, bytes_accessed=0, transcendentals=0),
        compiler_params=params(4),
    )(doubles)


def separate_kernel(pairs, out):
    rows = pairs.shape[0]
    out[:rows] = pairs[:, 0, :]
    out[rows:] = pairs[:, 1, :]


def separate(pairs):
    rows, count, width = pairs.shape
    return pl.pallas_call(
        separate_kernel,
        out_shape=jax.ShapeDtypeStruct((rows * count, width), pairs.dtype),
        in_specs=[VMEM],
        out_specs=VMEM,
        cost_estimate=pl.CostEstimate(flops=SEPARATE, bytes_accessed=0, transcendentals=0),
        compiler_params=params(4),
    )(pairs)


def keep_kernel(blocks, out, arrived):
    copy = pltpu.make_async_copy(blocks.at[lax.axis_index("stream")], out, arrived)
    copy.start()
    copy.wait()


def keep(blocks):
    return pl.pallas_call(
        keep_kernel,
        out_shape=jax.ShapeDtypeStruct(blocks.shape[1:], blocks.dtype),
        in_specs=[pl.BlockSpec(memory_space=pltpu.HBM)],
        out_specs=VMEM,
        scratch_shapes=[pltpu.SemaphoreType.DMA],
        compiler_params=params(1),
    )(in_hbm(blocks))


def choose_kernel(inside, relayed, out, arrived):
    row = lax.axis_index("vir") % 4

    def move(source):
        copy = pltpu.make_async_copy(source, out, arrived)
        copy.start()
        copy.wait()

    @pl.when(row != 0)
    def _():
        move(inside)

    @pl.when(row == 0)
    def _():
        move(relayed)


def choose(inside, relayed):
    return pl.pallas_call(
        choose_kernel,
        out_shape=jax.ShapeDtypeStruct(inside.shape, inside.dtype),
        in_specs=[ANYWHERE] * 2,
        out_specs=VMEM,
        scratch_shapes=[pltpu.SemaphoreType.DMA],
        compiler_params=params(1),
    )(inside, relayed)


def hold_kernel(*refs):
    pass


def hold(*values, flops):
    return pl.pallas_call(
        hold_kernel,
        out_shape=[jax.ShapeDtypeStruct(value.shape, value.dtype) for value in values],
        in_specs=[ANYWHERE] * len(values),
        out_specs=[ANYWHERE] * len(values),
        input_output_aliases={i: i for i in range(len(values))},
        cost_estimate=pl.CostEstimate(flops=flops, bytes_accessed=0, transcendentals=0),
        compiler_params=params(1),
    )(*values)


def multiply(picked, block):
    return lax.dot_general(picked, block, TRANSPOSED, preferred_element_type=jnp.float32)


def sum_call(kernel, dtype, flags, *operands):
    rows = operands[-1].shape[0]
    return pl.pallas_call(
        kernel,
        out_shape=jax.ShapeDtypeStruct((rows, 1024), dtype),
        in_specs=[SMEM] + [VMEM] * len(operands),
        out_specs=VMEM,
        cost_estimate=pl.CostEstimate(flops=0, bytes_accessed=0, transcendentals=0),
        compiler_params=params(12),
    )(flags, *operands)


def across_kernel(parity, kept, got, mine, other, out):
    core = lax.axis_index("stream")
    rows = mine.shape[0] // 2
    total = 0
    for holder, block in ((0, kept[1]), (1, got[core, 1])):
        second = parity[holder * 2 + 1] == 1
        halves = [jnp.where(second, half[rows:], half[:rows]) for half in (mine, other)]
        upper = jnp.where(core == 0, halves[0], halves[1])
        lower = jnp.where(core == 0, halves[1], halves[0])
        total = total + multiply(jnp.concatenate([upper, lower], 0), block)
    out[...] = total


def next_kernel(parity, kept, got, left, other_left, right, other_right, total, out):
    core = lax.axis_index("stream")
    result = total[...]
    for holder, block in ((0, kept[0]), (1, got[core, 0])):
        own = parity[holder * 2] == core
        picked = [
            jnp.where(own, held[...], swapped[...])
            for held, swapped in ((left, other_left), (right, other_right))
        ]
        result = result + multiply(jnp.concatenate(picked, 1), block)
    out[...] = result.astype(out.dtype)


def on_device(doubles, integrals, tiles):
    doubles, rows = lax.optimization_barrier((doubles, cut_rows(doubles)))
    across = send(rows, ACROSS)
    left, right = take(doubles)
    used = tiles[0, 0]
    parity = jnp.concatenate([used, swap(used)]) % 2
    relayed, parity = lax.optimization_barrier((send(right, RELAY_Y), parity))
    relayed = send(relayed, RELAY_X)
    inside = send(right, NEXT_INSIDE)
    first_left = send(left, NEXT)

    blocks, _ = lax.optimization_barrier((integrals[0, 0], rows))
    got = swap(blocks)
    kept = keep(blocks)
    across, inside, kept, got = lax.optimization_barrier((across, inside, kept, got))
    across = separate(across)
    total = sum_call(across_kernel, jnp.float32, parity, kept, got, across, swap(across))
    first_right = choose(inside, relayed)
    first_left, other_left = hold(first_left, swap(first_left), flops=HOLD)
    out = sum_call(
        next_kernel,
        jnp.bfloat16,
        parity,
        kept,
        got,
        first_left,
        other_left,
        first_right,
        swap(first_right),
        total,
    )
    return out[:, None]


def solution(mesh):
    placed = (
        P("occ", "vir", None),
        P("vir", "stream", None, None, None, None),
        P("vir", "stream", None),
    )
    return jax.shard_map(
        on_device,
        mesh=mesh,
        in_specs=placed,
        out_specs=P("occ", ("vir", "stream"), None),
        check_vma=False,
    )
```

```python
import functools

import jax
import jax.numpy as jnp
from jax import lax
from jax.experimental import pallas as pl
from jax.experimental.pallas import tpu as pltpu
from jax.sharding import PartitionSpec as P

SWAP = ((0, 1), (1, 0))
CUT = 256
SEPARATE = 2300 * 10**6
HOLD = 4600 * 10**6
TRANSPOSED = (((1,), (1,)), ((), ()))


def device(x, y, core):
    return ((x % 4) * 4 + y % 4) * 2 + core


def chips():
    return [(x, y) for x in range(4) for y in range(4)]


def route(pairs):
    return tuple((device(*a), device(*b)) for a, b in pairs)


ACROSS = route(((x, y, c), (x + 2, y, c)) for x, y in chips() for c in (0, 1))
INSIDE = route(((x, y, c), (x, y + 1, c)) for x, y in chips() for c in (0, 1) if y < 3)
WRAP = route(((x, 3, c), (x + 1, 0, c)) for x in range(4) for c in (0, 1))
RELAY_ROW = {0: 1, 1: 0}
RELAY_Y = route(((x, 3, c), (x, RELAY_ROW[c], c)) for x in range(4) for c in (0, 1))
RELAY_X = route(((x, RELAY_ROW[c], c), (x + 1, 0, c)) for x in range(4) for c in (0, 1))


def swap(value):
    return lax.ppermute(value, "stream", SWAP)


def send(value, pairs):
    return lax.ppermute(value, ("vir", "stream"), pairs)


VMEM = pl.BlockSpec(memory_space=pltpu.VMEM)
SMEM = pl.BlockSpec(memory_space=pltpu.SMEM)
ANYWHERE = pl.BlockSpec(memory_space=pl.ANY)


def params(mebibytes):
    return pltpu.CompilerParams(vmem_limit_bytes=mebibytes * 2**20)


def in_hbm(value):
    return pltpu.with_memory_space_constraint(value, pltpu.HBM)


def cut_kernel(doubles, out, arrived):
    rows = out.shape[0]
    core = lax.axis_index("stream")
    copy = pltpu.make_async_copy(doubles.at[pl.ds(core * rows, rows)], out, arrived)
    copy.start()
    copy.wait()


def cut_rows(doubles):
    shape = (doubles.shape[0] // 2, *doubles.shape[1:])
    return pl.pallas_call(
        cut_kernel,
        out_shape=jax.ShapeDtypeStruct(shape, doubles.dtype),
        in_specs=[pl.BlockSpec(memory_space=pltpu.HBM)],
        out_specs=VMEM,
        scratch_shapes=[pltpu.SemaphoreType.DMA],
        compiler_params=params(1),
    )(in_hbm(doubles))


def separate_kernel(pairs, out):
    rows = pairs.shape[0]
    out[:rows] = pairs[:, 0, :]
    out[rows:] = pairs[:, 1, :]


def separate_wrap_kernel(pairs, left, right):
    rows = pairs.shape[0]

    @pl.when(lax.axis_index("vir") % 4 == 3)
    def _():
        for pair in (0, 1):
            place = pl.ds(pair * rows, rows)
            left[place] = pairs[:, pair, :CUT]
            right[place] = pairs[:, pair, CUT:]


def separate_next_kernel(inside, direct, relayed, out):
    wrapped = lax.axis_index("vir") % 4 == 0

    @pl.when(jnp.logical_not(wrapped))
    def _():
        separate_kernel(inside, out)

    @pl.when(wrapped)
    def _():
        out[:, :CUT] = direct[...]
        out[:, CUT:] = relayed[...]


def separate(kernel, flops, widths, *operands):
    rows, count, _ = operands[0].shape
    return pl.pallas_call(
        kernel,
        out_shape=[
            jax.ShapeDtypeStruct((rows * count, width), operands[0].dtype) for width in widths
        ],
        in_specs=[VMEM] * len(operands),
        out_specs=[VMEM] * len(widths),
        cost_estimate=pl.CostEstimate(flops=flops, bytes_accessed=0, transcendentals=0),
        compiler_params=params(4),
    )(*operands)


def keep_kernel(blocks, out, arrived):
    copy = pltpu.make_async_copy(blocks.at[lax.axis_index("stream")], out, arrived)
    copy.start()
    copy.wait()


def keep(blocks):
    return pl.pallas_call(
        keep_kernel,
        out_shape=jax.ShapeDtypeStruct(blocks.shape[1:], blocks.dtype),
        in_specs=[pl.BlockSpec(memory_space=pltpu.HBM)],
        out_specs=VMEM,
        scratch_shapes=[pltpu.SemaphoreType.DMA],
        compiler_params=params(1),
    )(in_hbm(blocks))


def hold_kernel(*refs):
    pass


def hold(*values, flops):
    return pl.pallas_call(
        hold_kernel,
        out_shape=[jax.ShapeDtypeStruct(value.shape, value.dtype) for value in values],
        in_specs=[ANYWHERE] * len(values),
        out_specs=[ANYWHERE] * len(values),
        input_output_aliases={i: i for i in range(len(values))},
        cost_estimate=pl.CostEstimate(flops=flops, bytes_accessed=0, transcendentals=0),
        compiler_params=params(1),
    )(*values)


def multiply(picked, block):
    return lax.dot_general(picked, block, TRANSPOSED, preferred_element_type=jnp.float32)


def sum_kernel(slot, has_total, parity, kept, got, mine, other, *refs):
    out = refs[-1]
    core = lax.axis_index("stream")
    rows = mine.shape[0] // 2
    total = refs[0][...] if has_total else 0
    for holder, block in ((0, kept[slot]), (1, got[core, slot])):
        second = parity[holder * 2 + slot] == 1
        halves = [jnp.where(second, half[rows:], half[:rows]) for half in (mine, other)]
        upper = jnp.where(core == 0, halves[0], halves[1])
        lower = jnp.where(core == 0, halves[1], halves[0])
        total = total + multiply(jnp.concatenate([upper, lower], 0), block)
    out[...] = total.astype(out.dtype)


def add_slot(slot, dtype, parity, *operands):
    return pl.pallas_call(
        functools.partial(sum_kernel, slot, len(operands) == 5),
        out_shape=jax.ShapeDtypeStruct(operands[2].shape, dtype),
        in_specs=[SMEM] + [VMEM] * len(operands),
        out_specs=VMEM,
        cost_estimate=pl.CostEstimate(flops=0, bytes_accessed=0, transcendentals=0),
        compiler_params=params(12),
    )(parity, *operands)


def on_device(doubles, integrals, tiles):
    rows = cut_rows(doubles)
    across = send(rows, ACROSS)
    inside = send(rows, INSIDE)
    left, right = separate(separate_wrap_kernel, 0, (CUT, 1024 - CUT), rows)
    relayed = send(send(right, RELAY_Y), RELAY_X)
    direct = send(left, WRAP)

    blocks, _ = lax.optimization_barrier((integrals[0, 0], rows))
    got, tiles = lax.optimization_barrier((swap(blocks), tiles))
    kept = keep(blocks)
    used = tiles[0, 0]
    parity = jnp.concatenate([used, swap(used)]) % 2
    (across,) = separate(separate_kernel, SEPARATE, (1024,), across)
    across, inside, kept, got, parity = lax.optimization_barrier(
        (across, inside, kept, got, parity)
    )
    total = add_slot(1, jnp.float32, parity, kept, got, across, swap(across))
    (direct,) = hold(direct, flops=HOLD)
    (first,) = separate(separate_next_kernel, 0, (1024,), inside, direct, relayed)
    out = add_slot(0, jnp.bfloat16, parity, kept, got, first, swap(first), total)
    return out[:, None]


def solution(mesh):
    placed = (
        P("occ", "vir", None),
        P("vir", "stream", None, None, None, None),
        P("vir", "stream", None),
    )
    return jax.shard_map(
        on_device,
        mesh=mesh,
        in_specs=placed,
        out_specs=P("occ", ("vir", "stream"), None),
        check_vma=False,
    )
```

```python
import functools

import jax
import jax.numpy as jnp
from jax import lax
from jax.experimental import pallas as pl
from jax.experimental.pallas import tpu as pltpu
from jax.sharding import PartitionSpec as P

SWAP = ((0, 1), (1, 0))
CUT = 256
SEPARATE = 2300 * 10**6
HOLD = 4600 * 10**6
TRANSPOSED = (((1,), (1,)), ((), ()))


def device(x, y, core):
    return ((x % 4) * 4 + y % 4) * 2 + core


def chips():
    return [(x, y) for x in range(4) for y in range(4)]


def route(pairs):
    return tuple((device(*a), device(*b)) for a, b in pairs)


ACROSS = route(((x, y, c), (x + 2, y, c)) for x, y in chips() for c in (0, 1))
INSIDE = route(((x, y, c), (x, y + 1, c)) for x, y in chips() for c in (0, 1) if y < 3)
WRAP = route(((x, 3, c), (x + 1, 0, c)) for x in range(4) for c in (0, 1))
RELAY_ROW = {0: 1, 1: 0}
RELAY_Y = route(((x, 3, c), (x, RELAY_ROW[c], c)) for x in range(4) for c in (0, 1))
RELAY_X = route(((x, RELAY_ROW[c], c), (x + 1, 0, c)) for x in range(4) for c in (0, 1))


def swap(value):
    return lax.ppermute(value, "stream", SWAP)


def send(value, pairs):
    return lax.ppermute(value, ("vir", "stream"), pairs)


VMEM = pl.BlockSpec(memory_space=pltpu.VMEM)
SMEM = pl.BlockSpec(memory_space=pltpu.SMEM)
ANYWHERE = pl.BlockSpec(memory_space=pl.ANY)


def params(mebibytes):
    return pltpu.CompilerParams(vmem_limit_bytes=mebibytes * 2**20)


def in_hbm(value):
    return pltpu.with_memory_space_constraint(value, pltpu.HBM)


def cut_kernel(doubles, out, arrived):
    rows = out.shape[0]
    core = lax.axis_index("stream")
    copy = pltpu.make_async_copy(doubles.at[pl.ds(core * rows, rows)], out, arrived)
    copy.start()
    copy.wait()


def cut_rows(doubles):
    shape = (doubles.shape[0] // 2, *doubles.shape[1:])
    return pl.pallas_call(
        cut_kernel,
        out_shape=jax.ShapeDtypeStruct(shape, doubles.dtype),
        in_specs=[pl.BlockSpec(memory_space=pltpu.HBM)],
        out_specs=VMEM,
        scratch_shapes=[pltpu.SemaphoreType.DMA],
        compiler_params=params(1),
    )(in_hbm(doubles))


def separate_kernel(pairs, out):
    rows = pairs.shape[0]
    out[:rows] = pairs[:, 0, :]
    out[rows:] = pairs[:, 1, :]


def separate_wrap_kernel(low, pairs, out):
    rows, width = pairs.shape[0], out.shape[1]

    @pl.when(lax.axis_index("vir") % 4 == 3)
    def _():
        for pair in (0, 1):
            out[pl.ds(pair * rows, rows)] = pairs[:, pair, low : low + width]


def separate_next_kernel(inside, direct, relayed, out):
    wrapped = lax.axis_index("vir") % 4 == 0

    @pl.when(jnp.logical_not(wrapped))
    def _():
        separate_kernel(inside, out)

    @pl.when(wrapped)
    def _():
        out[:, :CUT] = direct[...]
        out[:, CUT:] = relayed[...]


def separate(kernel, flops, widths, *operands):
    rows, count, _ = operands[0].shape
    return pl.pallas_call(
        kernel,
        out_shape=[
            jax.ShapeDtypeStruct((rows * count, width), operands[0].dtype) for width in widths
        ],
        in_specs=[VMEM] * len(operands),
        out_specs=[VMEM] * len(widths),
        cost_estimate=pl.CostEstimate(flops=flops, bytes_accessed=0, transcendentals=0),
        compiler_params=params(4),
    )(*operands)


def keep_kernel(blocks, out, arrived):
    copy = pltpu.make_async_copy(blocks.at[lax.axis_index("stream")], out, arrived)
    copy.start()
    copy.wait()


def keep(blocks):
    return pl.pallas_call(
        keep_kernel,
        out_shape=jax.ShapeDtypeStruct(blocks.shape[1:], blocks.dtype),
        in_specs=[pl.BlockSpec(memory_space=pltpu.HBM)],
        out_specs=VMEM,
        scratch_shapes=[pltpu.SemaphoreType.DMA],
        compiler_params=params(1),
    )(in_hbm(blocks))


def hold_kernel(*refs):
    pass


def hold(*values, flops):
    return pl.pallas_call(
        hold_kernel,
        out_shape=[jax.ShapeDtypeStruct(value.shape, value.dtype) for value in values],
        in_specs=[ANYWHERE] * len(values),
        out_specs=[ANYWHERE] * len(values),
        input_output_aliases={i: i for i in range(len(values))},
        cost_estimate=pl.CostEstimate(flops=flops, bytes_accessed=0, transcendentals=0),
        compiler_params=params(1),
    )(*values)


def multiply(picked, block):
    return lax.dot_general(picked, block, TRANSPOSED, preferred_element_type=jnp.float32)


def picks(slot, parity, mine, other):
    core = lax.axis_index("stream")
    rows = mine.shape[0] // 2
    for holder in (0, 1):
        second = parity[holder * 2 + slot] == 1
        halves = [jnp.where(second, half[rows:], half[:rows]) for half in (mine, other)]
        upper = jnp.where(core == 0, halves[0], halves[1])
        lower = jnp.where(core == 0, halves[1], halves[0])
        yield jnp.concatenate([upper, lower], 0)


def across_kernel(parity, kept, got, mine, other, out):
    first, second = picks(1, parity, mine, other)
    core = lax.axis_index("stream")
    out[...] = multiply(first, kept[1]) + multiply(second, got[core, 1])


def next_kernel(parity, kept, got, mine, other, total, out, ready, sent):
    first, second = picks(0, parity, mine, other)
    core = lax.axis_index("stream")
    width = total.shape[1] // 2
    copies = []
    for i in (0, 1):
        place = pl.ds(i * width, width)
        result = total[:, place] + multiply(first, kept[0, place])
        result = result + multiply(second, got[core, 0, place])
        ready[:, place] = result.astype(ready.dtype)
        copies.append(pltpu.make_async_copy(ready.at[:, place], out.at[:, place], sent.at[i]))
        copies[i].start()
    for copy in copies:
        copy.wait()


def sum_call(kernel, dtype, out_spec, scratch, parity, *operands):
    return pl.pallas_call(
        kernel,
        out_shape=jax.ShapeDtypeStruct(operands[2].shape, dtype),
        in_specs=[SMEM] + [VMEM] * len(operands),
        out_specs=out_spec,
        scratch_shapes=scratch,
        cost_estimate=pl.CostEstimate(flops=0, bytes_accessed=0, transcendentals=0),
        compiler_params=params(12),
    )(parity, *operands)


def on_device(doubles, integrals, tiles):
    rows = cut_rows(doubles)
    across = send(rows, ACROSS)
    inside = send(rows, INSIDE)
    (right,) = separate(functools.partial(separate_wrap_kernel, CUT), 0, (1024 - CUT,), rows)
    (left,) = separate(functools.partial(separate_wrap_kernel, 0), 0, (CUT,), rows)
    relayed = send(send(right, RELAY_Y), RELAY_X)
    direct = send(left, WRAP)

    blocks, _ = lax.optimization_barrier((integrals[0, 0], rows))
    got, tiles = lax.optimization_barrier((swap(blocks), tiles))
    kept = keep(blocks)
    used = tiles[0, 0]
    parity = jnp.concatenate([used, swap(used)]) % 2
    (across,) = separate(separate_kernel, SEPARATE, (1024,), across)
    across, kept, got, parity = lax.optimization_barrier((across, kept, got, parity))
    total = sum_call(
        across_kernel, jnp.float32, VMEM, [], parity, kept, got, across, swap(across)
    )
    (direct,) = hold(direct, flops=HOLD)
    (first,) = separate(separate_next_kernel, 0, (1024,), inside, direct, relayed)
    scratch = [pltpu.VMEM(first.shape, jnp.bfloat16), pltpu.SemaphoreType.DMA((2,))]
    out = sum_call(
        next_kernel,
        jnp.bfloat16,
        ANYWHERE,
        scratch,
        parity,
        kept,
        got,
        first,
        swap(first),
        total,
    )
    return out[:, None]


def solution(mesh):
    placed = (
        P("occ", "vir", None),
        P("vir", "stream", None, None, None, None),
        P("vir", "stream", None),
    )
    return jax.shard_map(
        on_device,
        mesh=mesh,
        in_specs=placed,
        out_specs=P("occ", ("vir", "stream"), None),
        check_vma=False,
    )
```

```python
import functools

import jax
import jax.numpy as jnp
from jax import lax
from jax.experimental import pallas as pl
from jax.experimental.pallas import tpu as pltpu
from jax.sharding import PartitionSpec as P

SWAP = ((0, 1), (1, 0))
CUT = 256
SEPARATE = 6 * 1150 * 10**6
HOLD = 4600 * 10**6
TRANSPOSED = (((1,), (1,)), ((), ()))


def device(x, y, core):
    return ((x % 4) * 4 + y % 4) * 2 + core


def chips():
    return [(x, y) for x in range(4) for y in range(4)]


def route(pairs):
    return tuple((device(*a), device(*b)) for a, b in pairs)


ACROSS = route(((x, y, c), (x + 2, y, c)) for x, y in chips() for c in (0, 1))
INSIDE = route(((x, y, c), (x, y + 1, c)) for x, y in chips() for c in (0, 1) if y < 3)
WRAP = route(((x, 3, c), (x + 1, 0, c)) for x in range(4) for c in (0, 1))
RELAY_ROW = {0: 1, 1: 0}
RELAY_Y = route(((x, 3, c), (x, RELAY_ROW[c], c)) for x in range(4) for c in (0, 1))
RELAY_X = route(((x, RELAY_ROW[c], c), (x + 1, 0, c)) for x in range(4) for c in (0, 1))


def swap(value):
    return lax.ppermute(value, "stream", SWAP)


def send(value, pairs):
    return lax.ppermute(value, ("vir", "stream"), pairs)


VMEM = pl.BlockSpec(memory_space=pltpu.VMEM)
SMEM = pl.BlockSpec(memory_space=pltpu.SMEM)
ANYWHERE = pl.BlockSpec(memory_space=pl.ANY)


def params(mebibytes):
    return pltpu.CompilerParams(vmem_limit_bytes=mebibytes * 2**20)


def in_hbm(value):
    return pltpu.with_memory_space_constraint(value, pltpu.HBM)


def cut_kernel(doubles, out, arrived):
    rows = out.shape[0]
    core = lax.axis_index("stream")
    copy = pltpu.make_async_copy(doubles.at[pl.ds(core * rows, rows)], out, arrived)
    copy.start()
    copy.wait()


def cut_rows(doubles):
    shape = (doubles.shape[0] // 2, *doubles.shape[1:])
    return pl.pallas_call(
        cut_kernel,
        out_shape=jax.ShapeDtypeStruct(shape, doubles.dtype),
        in_specs=[pl.BlockSpec(memory_space=pltpu.HBM)],
        out_specs=VMEM,
        scratch_shapes=[pltpu.SemaphoreType.DMA],
        compiler_params=params(1),
    )(in_hbm(doubles))


def separate_kernel(pairs, out):
    rows = pairs.shape[0]
    out[:rows] = pairs[:, 0, :]
    out[rows:] = pairs[:, 1, :]


def separate_wrap_kernel(low, pairs, out):
    rows, width = pairs.shape[0], out.shape[1]

    @pl.when(lax.axis_index("vir") % 4 == 3)
    def _():
        for pair in (0, 1):
            out[pl.ds(pair * rows, rows)] = pairs[:, pair, low : low + width]


def separate_next_kernel(inside, direct, relayed, out):
    wrapped = lax.axis_index("vir") % 4 == 0

    @pl.when(jnp.logical_not(wrapped))
    def _():
        separate_kernel(inside, out)

    @pl.when(wrapped)
    def _():
        out[:, :CUT] = direct[...]
        out[:, CUT:] = relayed[...]


def separate(kernel, flops, widths, *operands):
    rows, count, _ = operands[0].shape
    return pl.pallas_call(
        kernel,
        out_shape=[
            jax.ShapeDtypeStruct((rows * count, width), operands[0].dtype) for width in widths
        ],
        in_specs=[VMEM] * len(operands),
        out_specs=[VMEM] * len(widths),
        cost_estimate=pl.CostEstimate(flops=flops, bytes_accessed=0, transcendentals=0),
        compiler_params=params(4),
    )(*operands)


def keep_kernel(blocks, out, arrived):
    copy = pltpu.make_async_copy(blocks.at[lax.axis_index("stream")], out, arrived)
    copy.start()
    copy.wait()


def keep(blocks):
    return pl.pallas_call(
        keep_kernel,
        out_shape=jax.ShapeDtypeStruct(blocks.shape[1:], blocks.dtype),
        in_specs=[pl.BlockSpec(memory_space=pltpu.HBM)],
        out_specs=VMEM,
        scratch_shapes=[pltpu.SemaphoreType.DMA],
        compiler_params=params(1),
    )(in_hbm(blocks))


def multiply(picked, block):
    return lax.dot_general(picked, block, TRANSPOSED, preferred_element_type=jnp.float32)


def picks(slot, parity, mine, other):
    core = lax.axis_index("stream")
    rows = mine.shape[0] // 2
    for holder in (0, 1):
        second = parity[holder * 2 + slot] == 1
        halves = [jnp.where(second, half[rows:], half[:rows]) for half in (mine, other)]
        upper = jnp.where(core == 0, halves[0], halves[1])
        lower = jnp.where(core == 0, halves[1], halves[0])
        yield jnp.concatenate([upper, lower], 0)


def across_kernel(parity, kept, got, mine, other, out):
    first, second = picks(1, parity, mine, other)
    core = lax.axis_index("stream")
    out[...] = multiply(first, kept[1]) + multiply(second, got[core, 1])


def next_kernel(parity, kept, got, mine, other, total, out, ready, sent):
    first, second = picks(0, parity, mine, other)
    core = lax.axis_index("stream")
    width = total.shape[1] // 2
    copies = []
    for i in (0, 1):
        place = pl.ds(i * width, width)
        result = total[:, place] + multiply(first, kept[0, place])
        result = result + multiply(second, got[core, 0, place])
        ready[:, place] = result.astype(ready.dtype)
        copies.append(pltpu.make_async_copy(ready.at[:, place], out.at[:, place], sent.at[i]))
        copies[i].start()
    for copy in copies:
        copy.wait()


def sum_call(kernel, dtype, out_spec, scratch, parity, *operands):
    return pl.pallas_call(
        kernel,
        out_shape=jax.ShapeDtypeStruct(operands[2].shape, dtype),
        in_specs=[SMEM] + [VMEM] * len(operands),
        out_specs=out_spec,
        scratch_shapes=scratch,
        cost_estimate=pl.CostEstimate(flops=0, bytes_accessed=0, transcendentals=0),
        compiler_params=params(12),
    )(parity, *operands)


def on_device(doubles, integrals, tiles):
    rows = cut_rows(doubles)
    across = send(rows, ACROSS)
    inside = send(rows, INSIDE)
    (right,) = separate(functools.partial(separate_wrap_kernel, CUT), 0, (1024 - CUT,), rows)
    (left,) = separate(functools.partial(separate_wrap_kernel, 0), 0, (CUT,), rows)
    relayed = send(send(right, RELAY_Y), RELAY_X)
    direct = send(left, WRAP)

    blocks, _ = lax.optimization_barrier((integrals[0, 0], rows))
    got, tiles = lax.optimization_barrier((swap(blocks), tiles))
    kept = keep(blocks)
    used = tiles[0, 0]
    parity = jnp.concatenate([used, swap(used)]) % 2
    (across,) = separate(separate_kernel, SEPARATE, (1024,), across)
    across, kept, got, parity = lax.optimization_barrier((across, kept, got, parity))
    total = sum_call(
        across_kernel, jnp.float32, VMEM, [], parity, kept, got, across, swap(across)
    )
    (first,) = separate(separate_next_kernel, HOLD, (1024,), inside, direct, relayed)
    scratch = [pltpu.VMEM(first.shape, jnp.bfloat16), pltpu.SemaphoreType.DMA((2,))]
    out = sum_call(
        next_kernel,
        jnp.bfloat16,
        ANYWHERE,
        scratch,
        parity,
        kept,
        got,
        first,
        swap(first),
        total,
    )
    return out[:, None]


def solution(mesh):
    placed = (
        P("occ", "vir", None),
        P("vir", "stream", None, None, None, None),
        P("vir", "stream", None),
    )
    return jax.shard_map(
        on_device,
        mesh=mesh,
        in_specs=placed,
        out_specs=P("occ", ("vir", "stream"), None),
        check_vma=False,
    )
```
